32 devices in a mesh: row: 4 (over y, x), col: 8 (over z, core).
Axes of the slice: x: 2, y: 2, z: 4, core: 2. Of those that a mesh axis runs over, the one named last changes fastest.
Arguments:
- features: bfloat16 [128, 1024, 256], P('row', 'col'), may hold values from -6 to 6
- conv_weight: bfloat16 [3, 3, 3, 256, 256], replicated, may hold values from -0.1875 to 0.1875
- conv_bias: float32 [3, 256], replicated, may hold values from -3 to 3
- boxes: int32 [4, 4, 8, 512], P(None, 'row', 'col'), may hold values from 0 to 256, as said below
- shards: int32 [4, 8, 512, 1], P('row', 'col'), may hold values from 0 to 31; in each aligned block of 512 rows (0 to 511, 512 to 1023, ..., all dimensions but the last counted through in order) at most 32 rows name the same one
- white_mean: float32 [256], replicated, may hold values from 0.2 to 1.5
- white_weight: bfloat16 [256, 1024], replicated, may hold values from -0.375 to 0.375
Outputs:
- index_rows: bfloat16 [32768, 1024], P(('row', 'col'))
The draws below stay inside these ranges and needn't reach their ends.
Inputs may be any that keep to these rules, and one draw needn't show every extreme that they name: Region k of the device at row index i and column index j has j * 32 <= boxes[2, i, j, k] < (j + 1) * 32; boxes[0] < boxes[1] <= 32, boxes[2] < boxes[3] <= 256, and boxes[3] - boxes[2] <= 32. `shards`: at most 32 regions of one device share a shard.
All inputs are finite; a program needn't handle non-finite values.
Results may differ from the reference program's by a relative error of at most 0.009.
Values may be sent and summed in bfloat16 or wider, within the bound.
A program may use at most 128 MiB of HBM per device.

```python
import math
import jax
import jax.numpy as jnp
import numpy as np
from jax import lax

C = 256
DESC = 1024
LAYERS = 3
BLK = 4
REG_DEV = 512
H = 128
W = 1024
TWB = 32
NBR = 32
NBC = 256
CAP = 32
N_ROW = 4
N_COL = 8
DEVICES = 32


def draw_boxes(key, part):
    key_rside, key_cside, key_row, key_col, key_deep = jax.random.split(key, 5)
    grid_shape = (N_ROW, N_COL, REG_DEV)
    is_first = (jnp.arange(REG_DEV) == 0)[None, None, :]
    row_side = jax.random.randint(key_rside, grid_shape, 1, NBR + 1)
    row_side = jnp.where(is_first, NBR, row_side)
    col_side = jax.random.randint(key_cside, grid_shape, 1, NBR + 1)
    deep_pick = jax.random.randint(key_deep, grid_shape, 0, 3) == 0
    deep_pick = deep_pick | is_first
    col_side = jnp.where(deep_pick, NBR, col_side)
    row_start = jax.random.randint(key_row, grid_shape, 0, NBR) % (NBR - row_side + 1)
    row_start = jnp.where(is_first, 0, row_start)
    offset = jax.random.randint(key_col, grid_shape, 0, TWB)
    offset = jnp.where(deep_pick, TWB - 1, offset)
    col_start = jnp.arange(N_COL)[None, :, None] * TWB + offset
    col_end = jnp.minimum(col_start + col_side, NBC)
    return jnp.stack([row_start, row_start + row_side, col_start, col_end]).astype(jnp.int32)


def level_of(key, shape, cuts, least, high):
    factor_of, own = 1.0, jax.random.fold_in(key, 6)
    for axis_at, blocks in cuts:
        heights = jnp.exp(jax.random.uniform(jax.random.fold_in(own, axis_at), (blocks,), jnp.float32, least / len(cuts), high / len(cuts)))
        factor_of = factor_of * jnp.repeat(heights, shape[axis_at] // blocks).reshape([-1 if axis == axis_at else 1 for axis in range(len(shape))])
    return factor_of


def deal_out(own_key, own, number, rows, amount, top, reach, slope):
    order = jax.random.permutation(own_key, amount)
    packed, usual = load_shares(amount, rows * top, reach, slope, True), load_shares(amount, rows * top, reach, slope, False)
    places = jnp.arange(amount)

    def named(tallies, offset_by):
        used = int((tallies > 0).sum())
        fixed = max(1, used // 4)
        shifted = fixed + (places - fixed + offset_by * (used - fixed)) % max(1, amount - fixed)
        return jnp.zeros((amount,), jnp.int32).at[order[jnp.where(places < fixed, places, shifted)]].set(jnp.asarray(tallies, jnp.int32))

    tallies = jnp.where(number % 4 == 0, named(packed, number // 4), named(usual, number - number // 4 - 1))
    mixed = jax.random.permutation(jax.random.fold_in(own, 3), amount)
    donor, sink = mixed[0:amount // 2 * 2:2], mixed[1:amount // 2 * 2:2]
    room = jnp.minimum(tallies[donor] - 1, reach - tallies[sink]) // 2
    room = jnp.where((donor == order[0]) | (sink == order[0]) | (tallies[sink] == 0), 0, jnp.maximum(room, 0))
    shifted = jax.random.randint(jax.random.fold_in(own, 4), (amount // 2,), 0, 1 << 20) % (room + 1)
    tallies = tallies.at[donor].add(-shifted).at[sink].add(shifted)
    members = jnp.searchsorted(jnp.cumsum(tallies), jnp.arange(rows * top), side="right").astype(jnp.int32)
    listing = members.reshape(top, rows).T
    listing = listing[jax.random.permutation(jax.random.fold_in(own, 1), rows)]
    offset_by = jax.random.randint(jax.random.fold_in(own, 2), (rows, 1), 0, top)
    return jnp.take_along_axis(listing, (jnp.arange(top)[None, :] + offset_by) % top, axis=1)


def load_shares(number_of, total, reach, skew, full):
    weights = [(1 << 20) // math.isqrt(standing ** skew) + 1 for standing in range(1, number_of + 1)]
    largest = reach if full else min(reach, max(-(-total // number_of), total * weights[0] // sum(weights)))
    least = 1 if total - largest >= number_of - 1 else 0
    holding, surplus = [largest] + [least] * (number_of - 1), total - largest - least * (number_of - 1)
    while surplus > 0:
        free = [i for i in range(1, number_of) if holding[i] < largest] or [i for i in range(1, number_of) if holding[i] < reach]
        pool, budget = sum([weights[i] for i in free]), surplus
        for i in free:
            addition = min(reach - holding[i], max(1, budget * weights[i] // pool), surplus)
            holding[i] = holding[i] + addition
            surplus = surplus - addition
    return np.array(holding)


def noise(stream_key, extent, deviation, limit, cuts=(), kind=jnp.bfloat16):
    array = jax.random.normal(stream_key, extent, jnp.float32) * deviation
    if len(cuts) > 0:
        array = level_of(stream_key, extent, cuts, -0.22, 0.18) * array
    return jnp.clip(array, min=-limit, max=limit).astype(kind)


def setup_inputs(seed: int = 0) -> dict:
    key_of = jax.random.split(jax.random.key(seed), 8)
    features = noise(key_of[0], (H, W, C), 1.0, 6.0, ((0, 4), (1, 8)))
    conv_weight = noise(key_of[1], (LAYERS, 3, 3, C, C), (9 * C // 2) ** -0.5, 0.1875)
    conv_bias = noise(key_of[2], (LAYERS, C), 0.5, 3.0, (), jnp.float32)
    boxes = draw_boxes(jax.random.fold_in(key_of[7], 71), 0)
    shards_keys = jax.random.split(jax.random.fold_in(key_of[4], 1), N_ROW * N_COL * REG_DEV // REG_DEV)
    shards_turns = jax.random.permutation(jax.random.fold_in(key_of[4], 3), N_ROW * N_COL * REG_DEV // REG_DEV)
    shards = jax.vmap(lambda own, number: deal_out(jax.random.fold_in(key_of[4], 2), own, number, REG_DEV, DEVICES, 1, CAP, 1))(shards_keys, shards_turns).reshape((N_ROW, N_COL, REG_DEV, 1))
    white_mean = jnp.clip(jax.random.uniform(key_of[5], (C,), jnp.float32, 0.2, 1.5), 0.2, 1.5)
    white_weight = noise(key_of[6], (C, DESC), C ** -0.5, 0.375)
    return {"features": features, "conv_weight": conv_weight, "conv_bias": conv_bias, "boxes": boxes, "shards": shards, "white_mean": white_mean, "white_weight": white_weight}


EPSILON = 1e-06

def conv_layer(padded, weights, biases):
    row_count = padded.shape[0] - 2
    col_count = padded.shape[1] - 2
    channels = padded.shape[2]
    running = jnp.zeros((row_count * col_count, weights.shape[3]), jnp.float32)
    for row_tap in range(3):
        for col_tap in range(3):
            window = padded[row_tap:row_tap + row_count, col_tap:col_tap + col_count, :].reshape(row_count * col_count, channels)
            running = running + jnp.dot(window, weights[row_tap, col_tap], preferred_element_type=jnp.float32)
    return jax.nn.relu(running + biases[None, :]).reshape(row_count, col_count, -1)

def block_max(hidden, block_side):
    row_count, col_count, channels = hidden.shape
    shaped = hidden.reshape(row_count // block_side, block_side, col_count // block_side, block_side, channels)
    return lax.optimization_barrier(jnp.max(shaped, axis=(1, 3)))

def pool_one(block_map, region_box, col_base):
    band_span = block_map.shape[0]
    start = (region_box[2] - col_base).astype(jnp.int32)
    window = lax.dynamic_slice(block_map, (jnp.int32(0), start, jnp.int32(0)), (band_span, band_span, block_map.shape[2]))
    positions = jnp.arange(band_span, dtype=jnp.int32)
    row_ok = (positions >= region_box[0]) & (positions < region_box[1])
    col_ok = positions < region_box[3] - region_box[2]
    inside = row_ok[:, None, None] & col_ok[None, :, None]
    return lax.optimization_barrier(jnp.max(jnp.where(inside, window, jnp.zeros((), window.dtype)), axis=(0, 1)))

def describe(pooled, white_mean, white_weight):
    values = pooled.astype(jnp.float32)
    unit_vec = values * lax.rsqrt(lax.optimization_barrier(jnp.mean(values * values, axis=-1, keepdims=True)) + EPSILON)
    centered = (unit_vec - white_mean[None, :]).astype(jnp.bfloat16)
    whitened = jnp.dot(centered, white_weight, preferred_element_type=jnp.float32)
    scaled = whitened * lax.rsqrt(lax.optimization_barrier(jnp.mean(whitened * whitened, axis=-1, keepdims=True)) + EPSILON)
    return scaled.astype(jnp.bfloat16)

def slot_rows(shard_ids, devices):
    onehot = (shard_ids[:, None] == jnp.arange(devices, dtype=jnp.int32)[None, :]).astype(jnp.int32)
    before = jnp.cumsum(onehot, axis=0) - onehot
    return lax.optimization_barrier(jnp.sum(before * onehot, axis=1)).astype(jnp.int32)

def reference(features, conv_weight, conv_bias, boxes, shards, white_mean, white_weight):
    hidden = features
    for layer_index in range(LAYERS):
        padded = jnp.pad(hidden, ((1, 1), (1, 1), (0, 0)))
        hidden = conv_layer(padded, conv_weight[layer_index], conv_bias[layer_index]).astype(jnp.bfloat16)
    block_map = block_max(hidden, BLK)
    extended = jnp.pad(block_map, ((0, 0), (0, NBR), (0, 0)))
    groups = boxes.reshape(4, -1).T.reshape(DEVICES, REG_DEV, 4)
    pooled = lax.map(lambda box_group: jax.vmap(lambda region_box: pool_one(extended, region_box, jnp.int32(0)))(box_group), groups)
    pooled = pooled.reshape(-1, C)
    descriptor = describe(pooled, white_mean, white_weight)
    shard_grid = shards.reshape(DEVICES, REG_DEV).astype(jnp.int32)
    slot_grid = jax.vmap(lambda shard_ids: slot_rows(shard_ids, DEVICES))(shard_grid)
    sources = jnp.arange(DEVICES, dtype=jnp.int32)[:, None]
    target = (shard_grid * (DEVICES * CAP) + sources * CAP + slot_grid).reshape(-1)
    output = jnp.zeros((DEVICES * DEVICES * CAP, DESC), jnp.bfloat16)
    return output.at[target].set(descriptor)
```

```python
import functools

import jax
import jax.numpy as jnp
from jax import lax
from jax.experimental import pallas as pl
from jax.experimental.pallas import tpu as pltpu
from jax.sharding import PartitionSpec as P

BLK = 4
EPSILON = 1e-06
PAD = 16
MESH = pl.DeviceIdType.MESH


def conv_kernel(n_row, n_col, feat, w, b, wide, a0, xa, xb, xc, load_sem, hs, hr, ms, mr):
    rows, cols, ch = feat.shape
    layers = w.shape[0]
    halo = layers
    wide_w = cols + 2 * PAD
    mid_w = xa.shape[1]
    brows = rows // BLK
    bcols = cols // BLK
    i = lax.axis_index("row")
    j = lax.axis_index("col")

    load = pltpu.make_async_copy(feat, a0.at[pl.ds(halo, rows), pl.ds(PAD, cols)], load_sem)
    load.start()

    barrier = pltpu.get_barrier_semaphore()
    for r in range(n_row):
        @pl.when(r != i)
        def _():
            pl.semaphore_signal(barrier, inc=1, device_id=(r, j), device_id_type=MESH)

        @pl.when(j > 0)
        def _():
            pl.semaphore_signal(barrier, inc=1, device_id=(r, jnp.maximum(j - 1, 0)), device_id_type=MESH)

        @pl.when(j < n_col - 1)
        def _():
            pl.semaphore_signal(barrier, inc=1, device_id=(r, jnp.minimum(j + 1, n_col - 1)), device_id_type=MESH)
    sides = jnp.where(j > 0, 1, 0) + jnp.where(j < n_col - 1, 1, 0)
    pl.semaphore_wait(barrier, n_row - 1 + n_row * sides)

    mid = pl.ds(halo, rows)
    to_left = pltpu.make_async_remote_copy(
        src_ref=feat.at[:, pl.ds(0, PAD)], dst_ref=a0.at[mid, pl.ds(PAD + cols, PAD)],
        send_sem=hs.at[0], recv_sem=hr.at[0],
        device_id=(i, jnp.maximum(j - 1, 0)), device_id_type=MESH)
    to_right = pltpu.make_async_remote_copy(
        src_ref=feat.at[:, pl.ds(cols - PAD, PAD)], dst_ref=a0.at[mid, pl.ds(0, PAD)],
        send_sem=hs.at[1], recv_sem=hr.at[1],
        device_id=(i, jnp.minimum(j + 1, n_col - 1)), device_id_type=MESH)
    to_up = pltpu.make_async_remote_copy(
        src_ref=a0.at[pl.ds(halo, halo)], dst_ref=a0.at[pl.ds(halo + rows, halo)],
        send_sem=hs.at[2], recv_sem=hr.at[2],
        device_id=(jnp.maximum(i - 1, 0), j), device_id_type=MESH)
    to_down = pltpu.make_async_remote_copy(
        src_ref=a0.at[pl.ds(rows, halo)], dst_ref=a0.at[pl.ds(0, halo)],
        send_sem=hs.at[3], recv_sem=hr.at[3],
        device_id=(jnp.minimum(i + 1, n_row - 1), j), device_id_type=MESH)

    @pl.when(j > 0)
    def _():
        to_left.start()

    @pl.when(j < n_col - 1)
    def _():
        to_right.start()

    @pl.when(j == 0)
    def _():
        a0[mid, 0:PAD, :] = jnp.zeros((rows, PAD, ch), a0.dtype)

    @pl.when(j == n_col - 1)
    def _():
        a0[mid, PAD + cols:wide_w, :] = jnp.zeros((rows, PAD, ch), a0.dtype)
        wide[:, bcols:2 * bcols, :] = jnp.zeros((wide.shape[0], bcols, ch), wide.dtype)

    @pl.when(i == 0)
    def _():
        a0[0:halo] = jnp.zeros((halo, wide_w, ch), a0.dtype)

    @pl.when(i == n_row - 1)
    def _():
        a0[halo + rows:2 * halo + rows] = jnp.zeros((halo, wide_w, ch), a0.dtype)

    load.wait()

    @pl.when(j < n_col - 1)
    def _():
        to_left.wait_recv()
        to_right.wait_send()

    @pl.when(j > 0)
    def _():
        to_right.wait_recv()
        to_left.wait_send()

    @pl.when(i > 0)
    def _():
        to_up.start()

    @pl.when(i < n_row - 1)
    def _():
        to_down.start()

    def spread(r):
        x = a0[r].astype(jnp.float32)
        for q in range(3):
            moved = pltpu.roll(x, wide_w - (PAD - halo) - q, 0)
            xa[r, :, q * ch:(q + 1) * ch] = moved[:mid_w].astype(xa.dtype)

    def taps(src, layer, r, count, width):
        acc = None
        for p in range(3):
            part = src[pl.ds(r + p, count), 0:width, :].reshape(count * width, 3 * ch)
            prod = jnp.dot(part, w[layer, p], preferred_element_type=jnp.float32)
            acc = prod if acc is None else acc + prod
        return jnp.maximum(acc + b[layer], 0.0)

    def inner(src, dst, layer, r, count, margin):
        y = taps(src, layer, r, count, mid_w)
        flat = lax.broadcasted_iota(jnp.int32, (count * mid_w, 1), 0)
        line = flat // mid_w
        row_at = r - margin + line
        col_at = flat - line * mid_w - margin
        ok = ((row_at >= 0) | (i > 0)) & ((row_at < rows) | (i < n_row - 1))
        ok = ok & ((col_at >= 0) | (j > 0)) & ((col_at < cols) | (j < n_col - 1))
        y = jnp.where(ok, y, 0.0)
        for q in range(3):
            moved = y if q == 0 else pltpu.roll(y, count * mid_w - q, 0)
            moved = moved.astype(dst.dtype).reshape(count, mid_w, ch)
            dst[pl.ds(r, count), :, q * ch:(q + 1) * ch] = moved[:, :dst.shape[1]]

    @pl.loop(halo, halo + rows)
    def _(r):
        spread(r)

    first = halo
    count1 = 3
    steps1 = (rows - 2) // count1

    @pl.loop(0, steps1)
    def _(s):
        inner(xa, xb, 0, first + s * count1, count1, 2)

    @pl.when(i < n_row - 1)
    def _():
        to_up.wait_recv()
        to_down.wait_send()

    @pl.when(i > 0)
    def _():
        to_down.wait_recv()
        to_up.wait_send()

    @pl.loop(0, halo)
    def _(r):
        spread(r)
        spread(r + halo + rows)

    @pl.loop(0, 2)
    def _(s):
        inner(xa, xb, 0, s * (rows + 1), count1, 2)

    @pl.loop(0, (rows + 2) // 4)
    def _(s):
        inner(xb, xc, 1, s * 4, 4, 1)

    inner(xb, xc, 1, rows, 2, 1)

    def move(bi, g, r):
        return pltpu.make_async_remote_copy(
            src_ref=wide.at[i * brows + bi, pl.ds(0, bcols)],
            dst_ref=wide.at[i * brows + bi, pl.ds(g * bcols, bcols)],
            send_sem=ms.at[bi, g * n_row + r], recv_sem=mr.at[bi, g * n_row + i],
            device_id=(r, j if g == 0 else jnp.maximum(j - 1, 0)), device_id_type=MESH)

    def arrive(bi, g, r):
        return pltpu.make_async_remote_copy(
            src_ref=wide.at[r * brows + bi, pl.ds(0, bcols)],
            dst_ref=wide.at[r * brows + bi, pl.ds(g * bcols, bcols)],
            send_sem=ms.at[bi, g * n_row + r], recv_sem=mr.at[bi, g * n_row + r],
            device_id=(r, j), device_id_type=MESH)

    @pl.loop(0, brows)
    def _(bi):
        y = taps(xc, 2, bi * BLK, BLK, cols)
        y = y.reshape(BLK, cols, ch)
        y = jnp.maximum(jnp.maximum(y[0], y[1]), jnp.maximum(y[2], y[3]))
        y = jnp.max(y.reshape(bcols, BLK, ch), axis=1)
        wide[i * brows + bi, 0:bcols, :] = y.astype(wide.dtype)
        for r in range(n_row):
            @pl.when(r != i)
            def _():
                move(bi, 0, r).start()

            @pl.when(j > 0)
            def _():
                move(bi, 1, r).start()

    @pl.loop(0, brows)
    def _(bi):
        for r in range(n_row):
            @pl.when(r != i)
            def _():
                move(bi, 0, r).wait_send()
                arrive(bi, 0, r).wait_recv()

            @pl.when(j > 0)
            def _():
                move(bi, 1, r).wait_send()

            @pl.when(j < n_col - 1)
            def _():
                arrive(bi, 1, r).wait_recv()


def pool_kernel(devices, capacity, boxes, shards, wide, out, table, part, lut):
    nrow, ncol2, ch = wide.shape
    halves = ch // 128
    regions = shards.shape[1]
    bcols = ncol2 // 2
    level_size = nrow * ncol2
    levels = table.shape[1] // level_size
    col_base = lax.axis_index("col") * bcols

    level = 0
    for size in range(1, nrow + 1):
        while 2 ** (level + 1) <= size:
            level += 1
        lut[0, size] = level * level_size
        lut[1, size] = level * level_size - (2 ** level) * ncol2

    @pl.loop(0, nrow)
    def _(r):
        x = wide[r].astype(jnp.float32)
        for h in range(halves):
            table[h, pl.ds(pl.multiple_of(r * ncol2, 8), ncol2), :] = x[:, h * 128:(h + 1) * 128]

    for lv in range(1, levels):
        step = 2 ** (lv - 1)
        below = (lv - 1) * level_size
        count = nrow - 2 ** lv + 1

        @pl.loop(0, count)
        def _(r):
            for h in range(halves):
                one = table[h, pl.ds(pl.multiple_of(below + r * ncol2, 8), ncol2), :]
                two = table[h, pl.ds(pl.multiple_of(below + (r + step) * ncol2, 8), ncol2), :]
                table[h, pl.ds(pl.multiple_of(below + level_size + r * ncol2, 8), ncol2), :] = (
                    jnp.maximum(one, two))

    sub = lax.broadcasted_iota(jnp.int32, (8, 128), 0)

    def pool(n):
        r0, r1, c0, c1 = (boxes[k, n] for k in range(4))
        span = jnp.maximum(r1 - r0, 1)
        c0 = jnp.maximum(c0 - col_base, 0)
        c1 = c1 - col_base
        high = lut[0, span] + r0 * ncol2
        low = jnp.maximum(lut[1, span] + r1 * ncol2, 0)
        last = jnp.maximum(c1 - 8, c0)
        starts = [c0, jnp.minimum(c0 + 8, last), jnp.minimum(c0 + 16, last), last]
        inside = sub < c1 - c0
        for h in range(halves):
            got = [table[h, pl.ds(base + c, 8), :] for base in (high, low) for c in starts]
            while len(got) > 1:
                got = [jnp.maximum(got[k], got[k + 1]) for k in range(0, len(got), 2)]
            part[h, pl.ds(pl.multiple_of(n * 8, 8), 8), :] = jnp.where(inside, got[0], 0.0)

    @pl.loop(0, regions // 4)
    def _(g):
        for k in range(4):
            pool(g * 4 + k)

    pooled = jnp.concatenate(
        [
            functools.reduce(
                jnp.maximum, [part[h, pl.ds(s, regions, stride=8), :] for s in range(8)])
            for h in range(halves)
        ],
        axis=1,
    ).astype(jnp.bfloat16)

    ids = shards[...]
    same = (lax.broadcasted_iota(jnp.int32, (devices, regions), 0) == ids).astype(jnp.float32)
    early = (lax.broadcasted_iota(jnp.int32, (regions, regions), 0)
             < lax.broadcasted_iota(jnp.int32, (regions, regions), 1)).astype(jnp.float32)
    before = jnp.dot(same.astype(jnp.bfloat16), early.astype(jnp.bfloat16),
                     preferred_element_type=jnp.float32)
    slot = jnp.sum(before * same, axis=0, keepdims=True)
    target = ids * capacity + slot.astype(jnp.int32)
    size = 256
    for s in range(devices * capacity // size):
        place = lax.broadcasted_iota(jnp.int32, (size, regions), 0) + s * size
        pick = (place == target).astype(jnp.float32)
        filled = jnp.sum(pick, axis=1, keepdims=True)
        moved = jnp.dot(pick.astype(jnp.bfloat16), pooled, preferred_element_type=jnp.float32)
        out[s * size:(s + 1) * size, :] = (moved + (filled - 1.0)).astype(out.dtype)


def scatter_kernel(n_row, n_col, src, dst, send_sem, recv_sem, own_sem):
    devices = n_row * n_col
    i = lax.axis_index("row")
    j = lax.axis_index("col")
    me = i * n_col + j
    own = pltpu.make_async_copy(src.at[me], dst.at[me], own_sem)
    own.start()
    barrier = pltpu.get_barrier_semaphore()

    @pl.loop(1, devices)
    def _(k):
        to = lax.rem(me + k, devices)
        pl.semaphore_signal(barrier, inc=1, device_id=(to // n_col, lax.rem(to, n_col)),
                            device_id_type=MESH)

    pl.semaphore_wait(barrier, devices - 1)

    def copy(k):
        to = lax.rem(me + k, devices)
        return pltpu.make_async_remote_copy(
            src_ref=src.at[to], dst_ref=dst.at[me],
            send_sem=send_sem.at[k], recv_sem=recv_sem.at[k],
            device_id=(to // n_col, lax.rem(to, n_col)), device_id_type=MESH)

    def got(k):
        away = lax.rem(me + devices - k, devices)
        return pltpu.make_async_remote_copy(
            src_ref=src.at[away], dst_ref=dst.at[away],
            send_sem=send_sem.at[k], recv_sem=recv_sem.at[k],
            device_id=(away // n_col, lax.rem(away, n_col)), device_id_type=MESH)

    @pl.loop(1, devices)
    def _(k):
        copy(k).start()

    own.wait()

    @pl.loop(1, devices)
    def _(k):
        copy(k).wait_send()
        got(k).wait_recv()


def describe_kernel(got, mean, weight, out):
    values = got[...].astype(jnp.float32)
    scale = lax.rsqrt(jnp.mean(values * values, axis=-1, keepdims=True) + EPSILON)
    centered = (values * scale - mean[...]).astype(jnp.bfloat16)
    white = jnp.dot(centered, weight[...], preferred_element_type=jnp.float32)
    scale = lax.rsqrt(jnp.mean(white * white, axis=-1, keepdims=True) + EPSILON)
    filled = values[:, 0:1] >= 0.0
    out[...] = jnp.where(filled, white * scale, 0.0).astype(out.dtype)


def body(n_row, n_col, features, conv_weight, conv_bias, boxes, shards, white_mean, white_weight):
    rows, cols, ch = features.shape
    layers = conv_weight.shape[0]
    devices = n_row * n_col
    regions = boxes.shape[-1]
    capacity = max(2, 2 * regions // devices)
    brows, bcols = rows // BLK, cols // BLK
    mid_w = cols + 16
    vmem = pl.BlockSpec(memory_space=pltpu.VMEM)
    any_spec = pl.BlockSpec(memory_space=pl.ANY)
    bf16 = jnp.bfloat16
    wide = pl.pallas_call(
        functools.partial(conv_kernel, n_row, n_col),
        out_shape=jax.ShapeDtypeStruct((n_row * brows, 2 * bcols, ch), bf16),
        in_specs=[any_spec, vmem, vmem],
        out_specs=vmem,
        scratch_shapes=[
            pltpu.VMEM((rows + 2 * layers, cols + 2 * PAD, ch), bf16),
            pltpu.VMEM((rows + 6, mid_w, 3 * ch), bf16),
            pltpu.VMEM((rows + 4, mid_w, 3 * ch), bf16),
            pltpu.VMEM((rows + 2, cols, 3 * ch), bf16),
            pltpu.SemaphoreType.DMA,
            pltpu.SemaphoreType.DMA((4,)),
            pltpu.SemaphoreType.DMA((4,)),
            pltpu.SemaphoreType.DMA((brows, 2 * n_row)),
            pltpu.SemaphoreType.DMA((brows, 2 * n_row)),
        ],
        compiler_params=pltpu.CompilerParams(
            collective_id=0, has_side_effects=True, vmem_limit_bytes=56 * 2**20),
    )(features, conv_weight.reshape(layers, 3, 3 * ch, ch), conv_bias.reshape(layers, 1, ch))

    nbr = n_row * brows
    levels = nbr.bit_length()
    outgoing = pl.pallas_call(
        functools.partial(pool_kernel, devices, capacity),
        out_shape=jax.ShapeDtypeStruct((devices * capacity, ch), bf16),
        in_specs=[pl.BlockSpec(memory_space=pltpu.SMEM), vmem, vmem],
        out_specs=vmem,
        scratch_shapes=[
            pltpu.VMEM((ch // 128, levels * nbr * 2 * bcols, 128), jnp.float32),
            pltpu.VMEM((ch // 128, regions * 8 + 8, 128), jnp.float32),
            pltpu.SMEM((2, nbr + 1), jnp.int32),
        ],
        compiler_params=pltpu.CompilerParams(vmem_limit_bytes=48 * 2**20),
    )(boxes.reshape(4, regions), shards.reshape(1, regions), wide)

    arrived = pl.pallas_call(
        functools.partial(scatter_kernel, n_row, n_col),
        out_shape=jax.ShapeDtypeStruct((devices, capacity, ch), bf16),
        in_specs=[vmem],
        out_specs=vmem,
        scratch_shapes=[
            pltpu.SemaphoreType.DMA((devices,)),
            pltpu.SemaphoreType.DMA((devices,)),
            pltpu.SemaphoreType.DMA,
        ],
        compiler_params=pltpu.CompilerParams(collective_id=1, has_side_effects=True),
    )(outgoing.reshape(devices, capacity, ch))

    total = devices * capacity
    desc = white_weight.shape[1]
    block = 256
    return pl.pallas_call(
        describe_kernel,
        grid=(total // block,),
        out_shape=jax.ShapeDtypeStruct((total, desc), bf16),
        in_specs=[
            pl.BlockSpec((block, ch), lambda s: (s, 0)),
            pl.BlockSpec((1, ch), lambda s: (0, 0)),
            pl.BlockSpec((ch, desc), lambda s: (0, 0)),
        ],
        out_specs=pl.BlockSpec((block, desc), lambda s: (s, 0)),
        compiler_params=pltpu.CompilerParams(vmem_limit_bytes=32 * 2**20),
    )(arrived.reshape(total, ch), white_mean.reshape(1, ch), white_weight)


def solution(mesh):
    in_specs = (
        P("row", "col", None),
        P(),
        P(),
        P(None, "row", "col", None),
        P("row", "col", None, None),
        P(),
        P(),
    )
    out_specs = P(("row", "col"), None)
    part = functools.partial(body, mesh.shape["row"], mesh.shape["col"])
    return jax.shard_map(part, mesh=mesh, in_specs=in_specs, out_specs=out_specs, check_vma=False)
```

```python
import functools

import jax
import jax.numpy as jnp
from jax import lax
from jax.experimental import pallas as pl
from jax.experimental.pallas import tpu as pltpu
from jax.sharding import PartitionSpec as P

BLK = 4
EPSILON = 1e-06
PAD = 16
MESH = pl.DeviceIdType.MESH


def conv_kernel(n_row, n_col, feat, w, b, wide, a0, xa, xb, xc, red, load_sem, hs, hr, ms, mr):
    rows, cols, ch = feat.shape
    layers = w.shape[0]
    halo = layers
    wide_w = cols + 2 * PAD
    mid_w = xa.shape[1]
    brows = rows // BLK
    bcols = cols // BLK
    i = lax.axis_index("row")
    j = lax.axis_index("col")

    load = pltpu.make_async_copy(feat, a0.at[pl.ds(halo, rows), pl.ds(PAD, cols)], load_sem)
    load.start()

    barrier = pltpu.get_barrier_semaphore()
    for r in range(n_row):
        @pl.when(r != i)
        def _():
            pl.semaphore_signal(barrier, inc=1, device_id=(r, j), device_id_type=MESH)

        @pl.when(j > 0)
        def _():
            pl.semaphore_signal(barrier, inc=1, device_id=(r, jnp.maximum(j - 1, 0)), device_id_type=MESH)

        @pl.when(j < n_col - 1)
        def _():
            pl.semaphore_signal(barrier, inc=1, device_id=(r, jnp.minimum(j + 1, n_col - 1)), device_id_type=MESH)
    sides = jnp.where(j > 0, 1, 0) + jnp.where(j < n_col - 1, 1, 0)
    pl.semaphore_wait(barrier, n_row - 1 + n_row * sides)

    mid = pl.ds(halo, rows)
    to_left = pltpu.make_async_remote_copy(
        src_ref=feat.at[:, pl.ds(0, PAD)], dst_ref=a0.at[mid, pl.ds(PAD + cols, PAD)],
        send_sem=hs.at[0], recv_sem=hr.at[0],
        device_id=(i, jnp.maximum(j - 1, 0)), device_id_type=MESH)
    to_right = pltpu.make_async_remote_copy(
        src_ref=feat.at[:, pl.ds(cols - PAD, PAD)], dst_ref=a0.at[mid, pl.ds(0, PAD)],
        send_sem=hs.at[1], recv_sem=hr.at[1],
        device_id=(i, jnp.minimum(j + 1, n_col - 1)), device_id_type=MESH)
    to_up = pltpu.make_async_remote_copy(
        src_ref=a0.at[pl.ds(halo, halo)], dst_ref=a0.at[pl.ds(halo + rows, halo)],
        send_sem=hs.at[2], recv_sem=hr.at[2],
        device_id=(jnp.maximum(i - 1, 0), j), device_id_type=MESH)
    to_down = pltpu.make_async_remote_copy(
        src_ref=a0.at[pl.ds(rows, halo)], dst_ref=a0.at[pl.ds(0, halo)],
        send_sem=hs.at[3], recv_sem=hr.at[3],
        device_id=(jnp.minimum(i + 1, n_row - 1), j), device_id_type=MESH)

    @pl.when(j > 0)
    def _():
        to_left.start()

    @pl.when(j < n_col - 1)
    def _():
        to_right.start()

    @pl.when(j == 0)
    def _():
        a0[mid, 0:PAD, :] = jnp.zeros((rows, PAD, ch), a0.dtype)

    @pl.when(j == n_col - 1)
    def _():
        a0[mid, PAD + cols:wide_w, :] = jnp.zeros((rows, PAD, ch), a0.dtype)
        wide[:, bcols:2 * bcols, :] = jnp.zeros((wide.shape[0], bcols, ch), wide.dtype)

    @pl.when(i == 0)
    def _():
        a0[0:halo] = jnp.zeros((halo, wide_w, ch), a0.dtype)

    @pl.when(i == n_row - 1)
    def _():
        a0[halo + rows:2 * halo + rows] = jnp.zeros((halo, wide_w, ch), a0.dtype)

    load.wait()

    @pl.when(j < n_col - 1)
    def _():
        to_left.wait_recv()
        to_right.wait_send()

    @pl.when(j > 0)
    def _():
        to_right.wait_recv()
        to_left.wait_send()

    @pl.when(i > 0)
    def _():
        to_up.start()

    @pl.when(i < n_row - 1)
    def _():
        to_down.start()

    col_at = lax.broadcasted_iota(jnp.int32, (mid_w, ch), 0)

    def spread(r):
        x = a0[r].astype(jnp.float32)
        for q in range(3):
            moved = pltpu.roll(x, wide_w - (PAD - halo) - q, 0)
            xa[r, :, q * ch:(q + 1) * ch] = moved[:mid_w].astype(xa.dtype)

    def taps(src, layer, r, count, width):
        acc = None
        for p in range(3):
            part = src[pl.ds(r + p, count), 0:width, :].reshape(count * width, 3 * ch)
            prod = jnp.dot(part, w[layer, p], preferred_element_type=jnp.float32)
            acc = prod if acc is None else acc + prod
        return jnp.maximum(acc + b[layer], 0.0)

    def inner(src, dst, layer, r, count, margin):
        y = taps(src, layer, r, count, mid_w)
        lines = []
        for k in range(count):
            row_at = r + k - margin
            row_ok = ((row_at >= 0) | (i > 0)) & ((row_at < rows) | (i < n_row - 1))
            low = jnp.where(j > 0, 0, margin)
            high = jnp.where(row_ok, jnp.where(j < n_col - 1, mid_w, cols + margin), 0)
            ok = (col_at >= low) & (col_at < high)
            lines.append(jnp.where(ok, y[k * mid_w:(k + 1) * mid_w], 0.0))
        y = jnp.concatenate(lines, axis=0)
        for q in range(3):
            moved = y if q == 0 else pltpu.roll(y, count * mid_w - q, 0)
            moved = moved.astype(dst.dtype).reshape(count, mid_w, ch)
            dst[pl.ds(r, count), :, q * ch:(q + 1) * ch] = moved[:, :dst.shape[1]]

    @pl.loop(halo, halo + rows)
    def _(r):
        spread(r)

    first = halo
    count1 = 3
    steps1 = (rows - 2) // count1

    @pl.loop(0, steps1)
    def _(s):
        inner(xa, xb, 0, first + s * count1, count1, 2)

    @pl.when(i < n_row - 1)
    def _():
        to_up.wait_recv()
        to_down.wait_send()

    @pl.when(i > 0)
    def _():
        to_down.wait_recv()
        to_up.wait_send()

    @pl.loop(0, halo)
    def _(r):
        spread(r)
        spread(r + halo + rows)

    @pl.loop(0, 2)
    def _(s):
        inner(xa, xb, 0, s * (rows + 1), count1, 2)

    @pl.loop(0, (rows + 2) // 4)
    def _(s):
        inner(xb, xc, 1, s * 4, 4, 1)

    inner(xb, xc, 1, rows, 2, 1)

    def move(bi, g, r):
        return pltpu.make_async_remote_copy(
            src_ref=wide.at[i * brows + bi, pl.ds(0, bcols)],
            dst_ref=wide.at[i * brows + bi, pl.ds(g * bcols, bcols)],
            send_sem=ms.at[bi, g * n_row + r], recv_sem=mr.at[bi, g * n_row + i],
            device_id=(r, j if g == 0 else jnp.maximum(j - 1, 0)), device_id_type=MESH)

    def arrive(bi, g, r):
        return pltpu.make_async_remote_copy(
            src_ref=wide.at[r * brows + bi, pl.ds(0, bcols)],
            dst_ref=wide.at[r * brows + bi, pl.ds(g * bcols, bcols)],
            send_sem=ms.at[bi, g * n_row + r], recv_sem=mr.at[bi, g * n_row + r],
            device_id=(r, j), device_id_type=MESH)

    @pl.loop(0, brows)
    def _(bi):
        y = taps(xc, 2, bi * BLK, BLK, cols)
        y = y.reshape(BLK, cols, ch)
        y = jnp.maximum(jnp.maximum(y[0], y[1]), jnp.maximum(y[2], y[3]))
        halves = []
        for h in range(ch // 128):
            red[h, 0:cols, :] = y[:, h * 128:(h + 1) * 128]
            parts = [red[h, pl.ds(k, bcols, stride=BLK), :] for k in range(BLK)]
            halves.append(functools.reduce(jnp.maximum, parts))
        wide[i * brows + bi, 0:bcols, :] = jnp.concatenate(halves, axis=1).astype(wide.dtype)
        for r in range(n_row):
            @pl.when(r != i)
            def _():
                move(bi, 0, r).start()

            @pl.when(j > 0)
            def _():
                move(bi, 1, r).start()

    @pl.loop(0, brows)
    def _(bi):
        for r in range(n_row):
            @pl.when(r != i)
            def _():
                move(bi, 0, r).wait_send()
                arrive(bi, 0, r).wait_recv()

            @pl.when(j > 0)
            def _():
                move(bi, 1, r).wait_send()

            @pl.when(j < n_col - 1)
            def _():
                arrive(bi, 1, r).wait_recv()


def pool_kernel(devices, capacity, boxes, shards, wide, out, table, part, lut):
    nrow, ncol2, ch = wide.shape
    halves = ch // 128
    regions = shards.shape[1]
    bcols = ncol2 // 2
    level_size = nrow * ncol2
    levels = table.shape[1] // level_size
    col_base = lax.axis_index("col") * bcols

    level = 0
    for size in range(1, nrow + 1):
        while 2 ** (level + 1) <= size:
            level += 1
        lut[0, size] = level * level_size
        lut[1, size] = level * level_size - (2 ** level) * ncol2

    @pl.loop(0, nrow)
    def _(r):
        x = wide[r].astype(jnp.float32)
        for h in range(halves):
            table[h, pl.ds(pl.multiple_of(r * ncol2, 8), ncol2), :] = x[:, h * 128:(h + 1) * 128]

    for lv in range(1, levels):
        step = 2 ** (lv - 1)
        below = (lv - 1) * level_size
        count = nrow - 2 ** lv + 1

        @pl.loop(0, count)
        def _(r):
            for h in range(halves):
                one = table[h, pl.ds(pl.multiple_of(below + r * ncol2, 8), ncol2), :]
                two = table[h, pl.ds(pl.multiple_of(below + (r + step) * ncol2, 8), ncol2), :]
                table[h, pl.ds(pl.multiple_of(below + level_size + r * ncol2, 8), ncol2), :] = (
                    jnp.maximum(one, two))

    sub = lax.broadcasted_iota(jnp.int32, (8, 128), 0)

    def pool(n):
        r0, r1, c0, c1 = (boxes[k, n] for k in range(4))
        span = jnp.maximum(r1 - r0, 1)
        c0 = jnp.maximum(c0 - col_base, 0)
        c1 = c1 - col_base
        high = lut[0, span] + r0 * ncol2
        low = jnp.maximum(lut[1, span] + r1 * ncol2, 0)
        last = jnp.maximum(c1 - 8, c0)
        starts = [c0, jnp.minimum(c0 + 8, last), jnp.minimum(c0 + 16, last), last]
        inside = sub < c1 - c0
        for h in range(halves):
            got = [table[h, pl.ds(base + c, 8), :] for base in (high, low) for c in starts]
            while len(got) > 1:
                got = [jnp.maximum(got[k], got[k + 1]) for k in range(0, len(got), 2)]
            part[h, pl.ds(pl.multiple_of(n * 8, 8), 8), :] = jnp.where(inside, got[0], 0.0)

    @pl.loop(0, regions // 4)
    def _(g):
        for k in range(4):
            pool(g * 4 + k)

    pooled = jnp.concatenate(
        [
            functools.reduce(
                jnp.maximum, [part[h, pl.ds(s, regions, stride=8), :] for s in range(8)])
            for h in range(halves)
        ],
        axis=1,
    ).astype(jnp.bfloat16)

    ids = shards[...]
    same = (lax.broadcasted_iota(jnp.int32, (devices, regions), 0) == ids).astype(jnp.float32)
    early = (lax.broadcasted_iota(jnp.int32, (regions, regions), 0)
             < lax.broadcasted_iota(jnp.int32, (regions, regions), 1)).astype(jnp.float32)
    before = jnp.dot(same.astype(jnp.bfloat16), early.astype(jnp.bfloat16),
                     preferred_element_type=jnp.float32)
    slot = jnp.sum(before * same, axis=0, keepdims=True)
    target = ids * capacity + slot.astype(jnp.int32)
    size = 256
    for s in range(devices * capacity // size):
        place = lax.broadcasted_iota(jnp.int32, (size, regions), 0) + s * size
        pick = (place == target).astype(jnp.float32)
        filled = jnp.sum(pick, axis=1, keepdims=True)
        moved = jnp.dot(pick.astype(jnp.bfloat16), pooled, preferred_element_type=jnp.float32)
        out[s * size:(s + 1) * size, :] = (moved + (filled - 1.0)).astype(out.dtype)


def scatter_kernel(n_row, n_col, src, dst, send_sem, recv_sem, own_sem):
    devices = n_row * n_col
    i = lax.axis_index("row")
    j = lax.axis_index("col")
    me = i * n_col + j
    own = pltpu.make_async_copy(src.at[me], dst.at[me], own_sem)
    own.start()
    barrier = pltpu.get_barrier_semaphore()

    @pl.loop(1, devices)
    def _(k):
        to = lax.rem(me + k, devices)
        pl.semaphore_signal(barrier, inc=1, device_id=(to // n_col, lax.rem(to, n_col)),
                            device_id_type=MESH)

    pl.semaphore_wait(barrier, devices - 1)

    def copy(k):
        to = lax.rem(me + k, devices)
        return pltpu.make_async_remote_copy(
            src_ref=src.at[to], dst_ref=dst.at[me],
            send_sem=send_sem.at[k], recv_sem=recv_sem.at[k],
            device_id=(to // n_col, lax.rem(to, n_col)), device_id_type=MESH)

    def got(k):
        away = lax.rem(me + devices - k, devices)
        return pltpu.make_async_remote_copy(
            src_ref=src.at[away], dst_ref=dst.at[away],
            send_sem=send_sem.at[k], recv_sem=recv_sem.at[k],
            device_id=(away // n_col, lax.rem(away, n_col)), device_id_type=MESH)

    @pl.loop(1, devices)
    def _(k):
        copy(k).start()

    own.wait()

    @pl.loop(1, devices)
    def _(k):
        copy(k).wait_send()
        got(k).wait_recv()


def describe_kernel(got, mean, weight, out):
    values = got[...].astype(jnp.float32)
    scale = lax.rsqrt(jnp.mean(values * values, axis=-1, keepdims=True) + EPSILON)
    centered = (values * scale - mean[...]).astype(jnp.bfloat16)
    white = jnp.dot(centered, weight[...], preferred_element_type=jnp.float32)
    scale = lax.rsqrt(jnp.mean(white * white, axis=-1, keepdims=True) + EPSILON)
    filled = values[:, 0:1] >= 0.0
    out[...] = jnp.where(filled, white * scale, 0.0).astype(out.dtype)


def body(n_row, n_col, features, conv_weight, conv_bias, boxes, shards, white_mean, white_weight):
    rows, cols, ch = features.shape
    layers = conv_weight.shape[0]
    devices = n_row * n_col
    regions = boxes.shape[-1]
    capacity = max(2, 2 * regions // devices)
    brows, bcols = rows // BLK, cols // BLK
    mid_w = cols + 16
    vmem = pl.BlockSpec(memory_space=pltpu.VMEM)
    any_spec = pl.BlockSpec(memory_space=pl.ANY)
    bf16 = jnp.bfloat16
    wide = pl.pallas_call(
        functools.partial(conv_kernel, n_row, n_col),
        out_shape=jax.ShapeDtypeStruct((n_row * brows, 2 * bcols, ch), bf16),
        in_specs=[any_spec, vmem, vmem],
        out_specs=vmem,
        scratch_shapes=[
            pltpu.VMEM((rows + 2 * layers, cols + 2 * PAD, ch), bf16),
            pltpu.VMEM((rows + 6, mid_w, 3 * ch), bf16),
            pltpu.VMEM((rows + 4, mid_w, 3 * ch), bf16),
            pltpu.VMEM((rows + 2, cols, 3 * ch), bf16),
            pltpu.VMEM((ch // 128, cols + 8, 128), jnp.float32),
            pltpu.SemaphoreType.DMA,
            pltpu.SemaphoreType.DMA((4,)),
            pltpu.SemaphoreType.DMA((4,)),
            pltpu.SemaphoreType.DMA((brows, 2 * n_row)),
            pltpu.SemaphoreType.DMA((brows, 2 * n_row)),
        ],
        compiler_params=pltpu.CompilerParams(
            collective_id=0, has_side_effects=True, vmem_limit_bytes=56 * 2**20),
    )(features, conv_weight.reshape(layers, 3, 3 * ch, ch), conv_bias.reshape(layers, 1, ch))

    nbr = n_row * brows
    levels = nbr.bit_length()
    outgoing = pl.pallas_call(
        functools.partial(pool_kernel, devices, capacity),
        out_shape=jax.ShapeDtypeStruct((devices * capacity, ch), bf16),
        in_specs=[pl.BlockSpec(memory_space=pltpu.SMEM), vmem, vmem],
        out_specs=vmem,
        scratch_shapes=[
            pltpu.VMEM((ch // 128, levels * nbr * 2 * bcols, 128), jnp.float32),
            pltpu.VMEM((ch // 128, regions * 8 + 8, 128), jnp.float32),
            pltpu.SMEM((2, nbr + 1), jnp.int32),
        ],
        compiler_params=pltpu.CompilerParams(vmem_limit_bytes=48 * 2**20),
    )(boxes.reshape(4, regions), shards.reshape(1, regions), wide)

    arrived = pl.pallas_call(
        functools.partial(scatter_kernel, n_row, n_col),
        out_shape=jax.ShapeDtypeStruct((devices, capacity, ch), bf16),
        in_specs=[vmem],
        out_specs=vmem,
        scratch_shapes=[
            pltpu.SemaphoreType.DMA((devices,)),
            pltpu.SemaphoreType.DMA((devices,)),
            pltpu.SemaphoreType.DMA,
        ],
        compiler_params=pltpu.CompilerParams(collective_id=1, has_side_effects=True),
    )(outgoing.reshape(devices, capacity, ch))

    total = devices * capacity
    desc = white_weight.shape[1]
    block = 256
    return pl.pallas_call(
        describe_kernel,
        grid=(total // block,),
        out_shape=jax.ShapeDtypeStruct((total, desc), bf16),
        in_specs=[
            pl.BlockSpec((block, ch), lambda s: (s, 0)),
            pl.BlockSpec((1, ch), lambda s: (0, 0)),
            pl.BlockSpec((ch, desc), lambda s: (0, 0)),
        ],
        out_specs=pl.BlockSpec((block, desc), lambda s: (s, 0)),
        compiler_params=pltpu.CompilerParams(vmem_limit_bytes=32 * 2**20),
    )(arrived.reshape(total, ch), white_mean.reshape(1, ch), white_weight)


def solution(mesh):
    in_specs = (
        P("row", "col", None),
        P(),
        P(),
        P(None, "row", "col", None),
        P("row", "col", None, None),
        P(),
        P(),
    )
    out_specs = P(("row", "col"), None)
    part = functools.partial(body, mesh.shape["row"], mesh.shape["col"])
    return jax.shard_map(part, mesh=mesh, in_specs=in_specs, out_specs=out_specs, check_vma=False)
```

```python
import functools

import jax
import jax.numpy as jnp
from jax import lax
from jax.experimental import pallas as pl
from jax.experimental.pallas import tpu as pltpu
from jax.sharding import PartitionSpec as P

BLK = 4
EPSILON = 1e-06
PAD = 16
MESH = pl.DeviceIdType.MESH


def conv_kernel(n_row, n_col, feat, w, b, wide, a0, xa, xb, xc, red, load_sem, hs, hr, ms, mr):
    rows, cols, ch = feat.shape
    layers = w.shape[0]
    halo = layers
    wide_w = cols + 2 * PAD
    mid_w = xa.shape[1]
    brows = rows // BLK
    bcols = cols // BLK
    i = lax.axis_index("row")
    j = lax.axis_index("col")

    load = pltpu.make_async_copy(feat, a0.at[pl.ds(halo, rows), pl.ds(PAD, cols)], load_sem)
    load.start()

    barrier = pltpu.get_barrier_semaphore()
    for r in range(n_row):
        @pl.when(r != i)
        def _():
            pl.semaphore_signal(barrier, inc=1, device_id=(r, j), device_id_type=MESH)

        @pl.when(j > 0)
        def _():
            pl.semaphore_signal(barrier, inc=1, device_id=(r, jnp.maximum(j - 1, 0)), device_id_type=MESH)

        @pl.when(j < n_col - 1)
        def _():
            pl.semaphore_signal(barrier, inc=1, device_id=(r, jnp.minimum(j + 1, n_col - 1)), device_id_type=MESH)
    sides = jnp.where(j > 0, 1, 0) + jnp.where(j < n_col - 1, 1, 0)
    pl.semaphore_wait(barrier, n_row - 1 + n_row * sides)

    mid = pl.ds(halo, rows)
    to_left = pltpu.make_async_remote_copy(
        src_ref=feat.at[:, pl.ds(0, PAD)], dst_ref=a0.at[mid, pl.ds(PAD + cols, PAD)],
        send_sem=hs.at[0], recv_sem=hr.at[0],
        device_id=(i, jnp.maximum(j - 1, 0)), device_id_type=MESH)
    to_right = pltpu.make_async_remote_copy(
        src_ref=feat.at[:, pl.ds(cols - PAD, PAD)], dst_ref=a0.at[mid, pl.ds(0, PAD)],
        send_sem=hs.at[1], recv_sem=hr.at[1],
        device_id=(i, jnp.minimum(j + 1, n_col - 1)), device_id_type=MESH)
    to_up = pltpu.make_async_remote_copy(
        src_ref=a0.at[pl.ds(halo, halo)], dst_ref=a0.at[pl.ds(halo + rows, halo)],
        send_sem=hs.at[2], recv_sem=hr.at[2],
        device_id=(jnp.maximum(i - 1, 0), j), device_id_type=MESH)
    to_down = pltpu.make_async_remote_copy(
        src_ref=a0.at[pl.ds(rows, halo)], dst_ref=a0.at[pl.ds(0, halo)],
        send_sem=hs.at[3], recv_sem=hr.at[3],
        device_id=(jnp.minimum(i + 1, n_row - 1), j), device_id_type=MESH)

    @pl.when(j > 0)
    def _():
        to_left.start()

    @pl.when(j < n_col - 1)
    def _():
        to_right.start()

    @pl.when(j == 0)
    def _():
        a0[mid, 0:PAD, :] = jnp.zeros((rows, PAD, ch), a0.dtype)

    @pl.when(j == n_col - 1)
    def _():
        a0[mid, PAD + cols:wide_w, :] = jnp.zeros((rows, PAD, ch), a0.dtype)
        wide[:, bcols:2 * bcols, :] = jnp.zeros((wide.shape[0], bcols, ch), wide.dtype)

    @pl.when(i == 0)
    def _():
        a0[0:halo] = jnp.zeros((halo, wide_w, ch), a0.dtype)

    @pl.when(i == n_row - 1)
    def _():
        a0[halo + rows:2 * halo + rows] = jnp.zeros((halo, wide_w, ch), a0.dtype)

    load.wait()

    @pl.when(j < n_col - 1)
    def _():
        to_left.wait_recv()
        to_right.wait_send()

    @pl.when(j > 0)
    def _():
        to_right.wait_recv()
        to_left.wait_send()

    @pl.when(i > 0)
    def _():
        to_up.start()

    @pl.when(i < n_row - 1)
    def _():
        to_down.start()

    col_at = lax.broadcasted_iota(jnp.int32, (mid_w, ch), 0)

    def spread(r):
        x = a0[r].astype(jnp.float32)
        for q in range(3):
            moved = pltpu.roll(x, wide_w - (PAD - halo) - q, 0)
            xa[r, :, q * ch:(q + 1) * ch] = moved[:mid_w].astype(xa.dtype)

    def taps(src, layer, r, count, width):
        acc = None
        for p in range(3):
            part = src[pl.ds(r + p, count), 0:width, :].reshape(count * width, 3 * ch)
            prod = jnp.dot(part, w[layer, p], preferred_element_type=jnp.float32)
            acc = prod if acc is None else acc + prod
        return jnp.maximum(acc + b[layer:layer + 1, :], 0.0)

    def inner(src, dst, layer, r, count, margin):
        y = taps(src, layer, r, count, mid_w)
        lines = []
        for k in range(count):
            row_at = r + k - margin
            row_ok = ((row_at >= 0) | (i > 0)) & ((row_at < rows) | (i < n_row - 1))
            low = jnp.where(j > 0, 0, margin)
            high = jnp.where(row_ok, jnp.where(j < n_col - 1, mid_w, cols + margin), 0)
            ok = (col_at >= low) & (col_at < high)
            lines.append(jnp.where(ok, y[k * mid_w:(k + 1) * mid_w], 0.0))
        y = jnp.concatenate(lines, axis=0)
        for q in range(3):
            moved = y if q == 0 else pltpu.roll(y, count * mid_w - q, 0)
            moved = moved.astype(dst.dtype).reshape(count, mid_w, ch)
            dst[pl.ds(r, count), :, q * ch:(q + 1) * ch] = moved[:, :dst.shape[1]]

    @pl.loop(halo, halo + rows)
    def _(r):
        spread(r)

    first = halo
    count1 = 3
    steps1 = (rows - 2) // count1

    @pl.loop(0, steps1)
    def _(s):
        inner(xa, xb, 0, first + s * count1, count1, 2)

    @pl.when(i < n_row - 1)
    def _():
        to_up.wait_recv()
        to_down.wait_send()

    @pl.when(i > 0)
    def _():
        to_down.wait_recv()
        to_up.wait_send()

    @pl.loop(0, halo)
    def _(r):
        spread(r)
        spread(r + halo + rows)

    @pl.loop(0, 2)
    def _(s):
        inner(xa, xb, 0, s * (rows + 1), count1, 2)

    @pl.loop(0, (rows + 2) // 4)
    def _(s):
        inner(xb, xc, 1, s * 4, 4, 1)

    inner(xb, xc, 1, rows, 2, 1)

    def move(bi, g, r):
        return pltpu.make_async_remote_copy(
            src_ref=wide.at[i * brows + bi, pl.ds(0, bcols)],
            dst_ref=wide.at[i * brows + bi, pl.ds(g * bcols, bcols)],
            send_sem=ms.at[bi, g * n_row + r], recv_sem=mr.at[bi, g * n_row + i],
            device_id=(r, j if g == 0 else jnp.maximum(j - 1, 0)), device_id_type=MESH)

    def arrive(bi, g, r):
        return pltpu.make_async_remote_copy(
            src_ref=wide.at[r * brows + bi, pl.ds(0, bcols)],
            dst_ref=wide.at[r * brows + bi, pl.ds(g * bcols, bcols)],
            send_sem=ms.at[bi, g * n_row + r], recv_sem=mr.at[bi, g * n_row + r],
            device_id=(r, j), device_id_type=MESH)

    @pl.loop(0, brows)
    def _(bi):
        y = taps(xc, 2, bi * BLK, BLK, cols)
        y = y.reshape(BLK, cols, ch)
        y = jnp.maximum(jnp.maximum(y[0], y[1]), jnp.maximum(y[2], y[3]))
        halves = []
        for h in range(ch // 128):
            red[h, 0:cols, :] = y[:, h * 128:(h + 1) * 128]
            parts = [red[h, pl.ds(k, bcols, stride=BLK), :] for k in range(BLK)]
            halves.append(functools.reduce(jnp.maximum, parts))
        wide[i * brows + bi, 0:bcols, :] = jnp.concatenate(halves, axis=1).astype(wide.dtype)
        for r in range(n_row):
            @pl.when(r != i)
            def _():
                move(bi, 0, r).start()

            @pl.when(j > 0)
            def _():
                move(bi, 1, r).start()

    @pl.loop(0, brows)
    def _(bi):
        for r in range(n_row):
            @pl.when(r != i)
            def _():
                move(bi, 0, r).wait_send()
                arrive(bi, 0, r).wait_recv()

            @pl.when(j > 0)
            def _():
                move(bi, 1, r).wait_send()

            @pl.when(j < n_col - 1)
            def _():
                arrive(bi, 1, r).wait_recv()


def pool_kernel(n_row, n_col, boxes, shards, wide, dst, src, table, part, lut,
                send_sem, recv_sem, own_sem):
    devices = n_row * n_col
    capacity = src.shape[1]
    me = lax.axis_index("row") * n_col + lax.axis_index("col")
    barrier = pltpu.get_barrier_semaphore()

    @pl.loop(1, devices)
    def _(k):
        to = lax.rem(me + k, devices)
        pl.semaphore_signal(barrier, inc=1, device_id=(to // n_col, lax.rem(to, n_col)),
                            device_id_type=MESH)

    nrow, ncol2, ch = wide.shape
    halves = ch // 128
    regions = shards.shape[1]
    bcols = ncol2 // 2
    level_size = nrow * ncol2
    levels = table.shape[1] // level_size
    col_base = lax.axis_index("col") * bcols

    level = 0
    for size in range(1, nrow + 1):
        while 2 ** (level + 1) <= size:
            level += 1
        lut[0, size] = level * level_size
        lut[1, size] = level * level_size - (2 ** level) * ncol2

    @pl.loop(0, nrow)
    def _(r):
        x = wide[r].astype(jnp.float32)
        for h in range(halves):
            table[h, pl.ds(pl.multiple_of(r * ncol2, 8), ncol2), :] = x[:, h * 128:(h + 1) * 128]

    for lv in range(1, levels):
        step = 2 ** (lv - 1)
        below = (lv - 1) * level_size
        count = nrow - 2 ** lv + 1

        @pl.loop(0, count)
        def _(r):
            for h in range(halves):
                one = table[h, pl.ds(pl.multiple_of(below + r * ncol2, 8), ncol2), :]
                two = table[h, pl.ds(pl.multiple_of(below + (r + step) * ncol2, 8), ncol2), :]
                table[h, pl.ds(pl.multiple_of(below + level_size + r * ncol2, 8), ncol2), :] = (
                    jnp.maximum(one, two))

    sub = lax.broadcasted_iota(jnp.int32, (8, 128), 0)

    def pool(n):
        r0, r1, c0, c1 = (boxes[k, n] for k in range(4))
        span = jnp.maximum(r1 - r0, 1)
        c0 = jnp.maximum(c0 - col_base, 0)
        c1 = c1 - col_base
        high = lut[0, span] + r0 * ncol2
        low = jnp.maximum(lut[1, span] + r1 * ncol2, 0)
        last = jnp.maximum(c1 - 8, c0)
        starts = [c0, jnp.minimum(c0 + 8, last), jnp.minimum(c0 + 16, last), last]
        inside = sub < c1 - c0
        for h in range(halves):
            got = [table[h, pl.ds(base + c, 8), :] for base in (high, low) for c in starts]
            while len(got) > 1:
                got = [jnp.maximum(got[k], got[k + 1]) for k in range(0, len(got), 2)]
            part[h, pl.ds(pl.multiple_of(n * 8, 8), 8), :] = jnp.where(inside, got[0], 0.0)

    @pl.loop(0, regions // 8)
    def _(g):
        for k in range(8):
            pool(g * 8 + k)

    pooled = jnp.concatenate(
        [
            functools.reduce(
                jnp.maximum, [part[h, pl.ds(s, regions, stride=8), :] for s in range(8)])
            for h in range(halves)
        ],
        axis=1,
    ).astype(jnp.bfloat16)

    ids = shards[...]
    same = (lax.broadcasted_iota(jnp.int32, (devices, regions), 0) == ids).astype(jnp.float32)
    early = (lax.broadcasted_iota(jnp.int32, (regions, regions), 0)
             < lax.broadcasted_iota(jnp.int32, (regions, regions), 1)).astype(jnp.float32)
    before = jnp.dot(same.astype(jnp.bfloat16), early.astype(jnp.bfloat16),
                     preferred_element_type=jnp.float32)
    slot = jnp.sum(before * same, axis=0, keepdims=True)
    target = ids * capacity + slot.astype(jnp.int32)
    size = 256
    for s in range(devices * capacity // size):
        place = lax.broadcasted_iota(jnp.int32, (size, regions), 0) + s * size
        pick = (place == target).astype(jnp.float32)
        filled = jnp.sum(pick, axis=1, keepdims=True)
        moved = jnp.dot(pick.astype(jnp.bfloat16), pooled, preferred_element_type=jnp.float32)
        moved = (moved + (filled - 1.0)).astype(src.dtype)
        group = size // capacity
        src[s * group:(s + 1) * group] = moved.reshape(group, capacity, ch)

    own = pltpu.make_async_copy(src.at[me], dst.at[me], own_sem)
    own.start()
    pl.semaphore_wait(barrier, devices - 1)

    def copy(k):
        to = lax.rem(me + k, devices)
        return pltpu.make_async_remote_copy(
            src_ref=src.at[to], dst_ref=dst.at[me],
            send_sem=send_sem.at[k], recv_sem=recv_sem.at[k],
            device_id=(to // n_col, lax.rem(to, n_col)), device_id_type=MESH)

    def got(k):
        away = lax.rem(me + devices - k, devices)
        return pltpu.make_async_remote_copy(
            src_ref=src.at[away], dst_ref=dst.at[away],
            send_sem=send_sem.at[k], recv_sem=recv_sem.at[k],
            device_id=(away // n_col, lax.rem(away, n_col)), device_id_type=MESH)

    @pl.loop(1, devices)
    def _(k):
        copy(k).start()

    own.wait()

    @pl.loop(1, devices)
    def _(k):
        copy(k).wait_send()
        got(k).wait_recv()


def describe_kernel(got, mean, weight, out):
    values = got[...].astype(jnp.float32)
    scale = lax.rsqrt(jnp.mean(values * values, axis=-1, keepdims=True) + EPSILON)
    centered = (values * scale - mean[...]).astype(jnp.bfloat16)
    white = jnp.dot(centered, weight[...], preferred_element_type=jnp.float32)
    scale = lax.rsqrt(jnp.mean(white * white, axis=-1, keepdims=True) + EPSILON)
    filled = values[:, 0:1] >= 0.0
    out[...] = jnp.where(filled, white * scale, 0.0).astype(out.dtype)


def body(n_row, n_col, features, conv_weight, conv_bias, boxes, shards, white_mean, white_weight):
    rows, cols, ch = features.shape
    layers = conv_weight.shape[0]
    devices = n_row * n_col
    regions = boxes.shape[-1]
    capacity = max(2, 2 * regions // devices)
    brows, bcols = rows // BLK, cols // BLK
    mid_w = cols + 16
    vmem = pl.BlockSpec(memory_space=pltpu.VMEM)
    any_spec = pl.BlockSpec(memory_space=pl.ANY)
    bf16 = jnp.bfloat16
    wide = pl.pallas_call(
        functools.partial(conv_kernel, n_row, n_col),
        out_shape=jax.ShapeDtypeStruct((n_row * brows, 2 * bcols, ch), bf16),
        in_specs=[any_spec, vmem, vmem],
        out_specs=vmem,
        scratch_shapes=[
            pltpu.VMEM((rows + 2 * layers, cols + 2 * PAD, ch), bf16),
            pltpu.VMEM((rows + 6, mid_w, 3 * ch), bf16),
            pltpu.VMEM((rows + 4, mid_w, 3 * ch), bf16),
            pltpu.VMEM((rows + 2, cols, 3 * ch), bf16),
            pltpu.VMEM((ch // 128, cols + 8, 128), jnp.float32),
            pltpu.SemaphoreType.DMA,
            pltpu.SemaphoreType.DMA((4,)),
            pltpu.SemaphoreType.DMA((4,)),
            pltpu.SemaphoreType.DMA((brows, 2 * n_row)),
            pltpu.SemaphoreType.DMA((brows, 2 * n_row)),
        ],
        compiler_params=pltpu.CompilerParams(
            collective_id=0, has_side_effects=True, vmem_limit_bytes=56 * 2**20),
    )(features, conv_weight.reshape(layers, 3, 3 * ch, ch), conv_bias)

    nbr = n_row * brows
    levels = nbr.bit_length()
    arrived = pl.pallas_call(
        functools.partial(pool_kernel, n_row, n_col),
        out_shape=jax.ShapeDtypeStruct((devices, capacity, ch), bf16),
        in_specs=[pl.BlockSpec(memory_space=pltpu.SMEM), vmem, vmem],
        out_specs=vmem,
        scratch_shapes=[
            pltpu.VMEM((devices, capacity, ch), bf16),
            pltpu.VMEM((ch // 128, levels * nbr * 2 * bcols, 128), jnp.float32),
            pltpu.VMEM((ch // 128, regions * 8 + 8, 128), jnp.float32),
            pltpu.SMEM((2, nbr + 1), jnp.int32),
            pltpu.SemaphoreType.DMA((devices,)),
            pltpu.SemaphoreType.DMA((devices,)),
            pltpu.SemaphoreType.DMA,
        ],
        compiler_params=pltpu.CompilerParams(
            collective_id=1, has_side_effects=True, vmem_limit_bytes=48 * 2**20),
    )(boxes.reshape(4, regions), shards.reshape(1, regions), wide)

    total = devices * capacity
    desc = white_weight.shape[1]
    block = 256
    return pl.pallas_call(
        describe_kernel,
        grid=(total // block,),
        out_shape=jax.ShapeDtypeStruct((total, desc), bf16),
        in_specs=[
            pl.BlockSpec((block, ch), lambda s: (s, 0)),
            pl.BlockSpec((1, ch), lambda s: (0, 0)),
            pl.BlockSpec((ch, desc), lambda s: (0, 0)),
        ],
        out_specs=pl.BlockSpec((block, desc), lambda s: (s, 0)),
        compiler_params=pltpu.CompilerParams(vmem_limit_bytes=32 * 2**20),
    )(arrived.reshape(total, ch), white_mean.reshape(1, ch), white_weight)


def solution(mesh):
    in_specs = (
        P("row", "col", None),
        P(),
        P(),
        P(None, "row", "col", None),
        P("row", "col", None, None),
        P(),
        P(),
    )
    out_specs = P(("row", "col"), None)
    part = functools.partial(body, mesh.shape["row"], mesh.shape["col"])
    return jax.shard_map(part, mesh=mesh, in_specs=in_specs, out_specs=out_specs, check_vma=False)
```

```python
import functools

import jax
import jax.numpy as jnp
from jax import lax
from jax.experimental import pallas as pl
from jax.experimental.pallas import tpu as pltpu
from jax.sharding import PartitionSpec as P

BLK = 4
EPSILON = 1e-06
PAD = 16
MESH = pl.DeviceIdType.MESH


def conv_kernel(n_row, n_col, feat, w, b, wide, a0, xa, xb, xc, red, load_sem, hs, hr, ms, mr):
    rows, cols, ch = feat.shape
    layers = w.shape[0]
    halo = layers
    wide_w = cols + 2 * PAD
    mid_w = xa.shape[1]
    brows = rows // BLK
    bcols = cols // BLK
    i = lax.axis_index("row")
    j = lax.axis_index("col")

    load = pltpu.make_async_copy(feat, a0.at[pl.ds(halo, rows), pl.ds(PAD, cols)], load_sem)
    load.start()

    barrier = pltpu.get_barrier_semaphore()
    for r in range(n_row):
        @pl.when(r != i)
        def _():
            pl.semaphore_signal(barrier, inc=1, device_id=(r, j), device_id_type=MESH)

        @pl.when(j > 0)
        def _():
            pl.semaphore_signal(barrier, inc=1, device_id=(r, jnp.maximum(j - 1, 0)), device_id_type=MESH)

        @pl.when(j < n_col - 1)
        def _():
            pl.semaphore_signal(barrier, inc=1, device_id=(r, jnp.minimum(j + 1, n_col - 1)), device_id_type=MESH)
    sides = jnp.where(j > 0, 1, 0) + jnp.where(j < n_col - 1, 1, 0)
    pl.semaphore_wait(barrier, n_row - 1 + n_row * sides)

    mid = pl.ds(halo, rows)
    to_left = pltpu.make_async_remote_copy(
        src_ref=feat.at[:, pl.ds(0, PAD)], dst_ref=a0.at[mid, pl.ds(PAD + cols, PAD)],
        send_sem=hs.at[0], recv_sem=hr.at[0],
        device_id=(i, jnp.maximum(j - 1, 0)), device_id_type=MESH)
    to_right = pltpu.make_async_remote_copy(
        src_ref=feat.at[:, pl.ds(cols - PAD, PAD)], dst_ref=a0.at[mid, pl.ds(0, PAD)],
        send_sem=hs.at[1], recv_sem=hr.at[1],
        device_id=(i, jnp.minimum(j + 1, n_col - 1)), device_id_type=MESH)
    to_up = pltpu.make_async_remote_copy(
        src_ref=a0.at[pl.ds(halo, halo)], dst_ref=a0.at[pl.ds(halo + rows, halo)],
        send_sem=hs.at[2], recv_sem=hr.at[2],
        device_id=(jnp.maximum(i - 1, 0), j), device_id_type=MESH)
    to_down = pltpu.make_async_remote_copy(
        src_ref=a0.at[pl.ds(rows, halo)], dst_ref=a0.at[pl.ds(0, halo)],
        send_sem=hs.at[3], recv_sem=hr.at[3],
        device_id=(jnp.minimum(i + 1, n_row - 1), j), device_id_type=MESH)

    @pl.when(j > 0)
    def _():
        to_left.start()

    @pl.when(j < n_col - 1)
    def _():
        to_right.start()

    @pl.when(j == 0)
    def _():
        a0[mid, 0:PAD, :] = jnp.zeros((rows, PAD, ch), a0.dtype)

    @pl.when(j == n_col - 1)
    def _():
        a0[mid, PAD + cols:wide_w, :] = jnp.zeros((rows, PAD, ch), a0.dtype)
        wide[:, bcols:2 * bcols, :] = jnp.zeros((wide.shape[0], bcols, ch), wide.dtype)

    @pl.when(i == 0)
    def _():
        a0[0:halo] = jnp.zeros((halo, wide_w, ch), a0.dtype)

    @pl.when(i == n_row - 1)
    def _():
        a0[halo + rows:2 * halo + rows] = jnp.zeros((halo, wide_w, ch), a0.dtype)

    load.wait()

    @pl.when(j < n_col - 1)
    def _():
        to_left.wait_recv()
        to_right.wait_send()

    @pl.when(j > 0)
    def _():
        to_right.wait_recv()
        to_left.wait_send()

    @pl.when(i > 0)
    def _():
        to_up.start()

    @pl.when(i < n_row - 1)
    def _():
        to_down.start()

    col_at = lax.broadcasted_iota(jnp.int32, (mid_w, ch), 0)

    def spread(r):
        x = a0[r].astype(jnp.float32)
        for q in range(3):
            moved = pltpu.roll(x, wide_w - (PAD - halo) - q, 0)
            xa[r, :, q * ch:(q + 1) * ch] = moved[:mid_w].astype(xa.dtype)

    def taps(src, layer, r, count, width):
        acc = None
        for p in range(3):
            part = src[pl.ds(r + p, count), 0:width, :].reshape(count * width, 3 * ch)
            prod = jnp.dot(part, w[layer, p], preferred_element_type=jnp.float32)
            acc = prod if acc is None else acc + prod
        return jnp.maximum(acc + b[layer:layer + 1, :], 0.0)

    def inner(src, dst, layer, r, count, margin):
        y = taps(src, layer, r, count, mid_w)
        lines = []
        for k in range(count):
            row_at = r + k - margin
            row_ok = ((row_at >= 0) | (i > 0)) & ((row_at < rows) | (i < n_row - 1))
            low = jnp.where(j > 0, 0, margin)
            high = jnp.where(row_ok, jnp.where(j < n_col - 1, mid_w, cols + margin), 0)
            ok = (col_at >= low) & (col_at < high)
            lines.append(jnp.where(ok, y[k * mid_w:(k + 1) * mid_w], 0.0))
        y = jnp.concatenate(lines, axis=0)
        for q in range(3):
            moved = y if q == 0 else pltpu.roll(y, count * mid_w - q, 0)
            moved = moved.astype(dst.dtype).reshape(count, mid_w, ch)
            dst[pl.ds(r, count), :, q * ch:(q + 1) * ch] = moved[:, :dst.shape[1]]

    @pl.loop(0, rows // 4)
    def _(g):
        for k in range(4):
            spread(halo + g * 4 + k)

    first = halo
    count1 = 6
    steps1 = (rows - 2) // count1

    @pl.loop(0, steps1)
    def _(s):
        inner(xa, xb, 0, first + s * count1, count1, 2)

    @pl.when(i < n_row - 1)
    def _():
        to_up.wait_recv()
        to_down.wait_send()

    @pl.when(i > 0)
    def _():
        to_down.wait_recv()
        to_up.wait_send()

    @pl.loop(0, halo)
    def _(r):
        spread(r)
        spread(r + halo + rows)

    @pl.loop(0, 2)
    def _(s):
        inner(xa, xb, 0, s * (rows + 1), halo, 2)

    @pl.loop(0, (rows + 2) // 4)
    def _(s):
        inner(xb, xc, 1, s * 4, 4, 1)

    inner(xb, xc, 1, rows, 2, 1)

    def move(bi, g, r):
        return pltpu.make_async_remote_copy(
            src_ref=wide.at[i * brows + bi, pl.ds(0, bcols)],
            dst_ref=wide.at[i * brows + bi, pl.ds(g * bcols, bcols)],
            send_sem=ms.at[bi, g * n_row + r], recv_sem=mr.at[bi, g * n_row + i],
            device_id=(r, j if g == 0 else jnp.maximum(j - 1, 0)), device_id_type=MESH)

    def arrive(bi, g, r):
        return pltpu.make_async_remote_copy(
            src_ref=wide.at[r * brows + bi, pl.ds(0, bcols)],
            dst_ref=wide.at[r * brows + bi, pl.ds(g * bcols, bcols)],
            send_sem=ms.at[bi, g * n_row + r], recv_sem=mr.at[bi, g * n_row + r],
            device_id=(r, j), device_id_type=MESH)

    @pl.loop(0, brows)
    def _(bi):
        y = taps(xc, 2, bi * BLK, BLK, cols)
        y = y.reshape(BLK, cols, ch)
        y = jnp.maximum(jnp.maximum(y[0], y[1]), jnp.maximum(y[2], y[3]))
        halves = []
        for h in range(ch // 128):
            red[h, 0:cols, :] = y[:, h * 128:(h + 1) * 128]
            parts = [red[h, pl.ds(k, bcols, stride=BLK), :] for k in range(BLK)]
            halves.append(functools.reduce(jnp.maximum, parts))
        wide[i * brows + bi, 0:bcols, :] = jnp.concatenate(halves, axis=1).astype(wide.dtype)
        for r in range(n_row):
            @pl.when(r != i)
            def _():
                move(bi, 0, r).start()

            @pl.when(j > 0)
            def _():
                move(bi, 1, r).start()

    @pl.loop(0, brows)
    def _(bi):
        for r in range(n_row):
            @pl.when(r != i)
            def _():
                move(bi, 0, r).wait_send()
                arrive(bi, 0, r).wait_recv()

            @pl.when(j > 0)
            def _():
                move(bi, 1, r).wait_send()

            @pl.when(j < n_col - 1)
            def _():
                arrive(bi, 1, r).wait_recv()


def pool_kernel(n_row, n_col, boxes, shards, wide, dst, src, table, part, lut,
                send_sem, recv_sem, own_sem):
    devices = n_row * n_col
    capacity = src.shape[1]
    me = lax.axis_index("row") * n_col + lax.axis_index("col")
    barrier = pltpu.get_barrier_semaphore()

    @pl.loop(1, devices)
    def _(k):
        to = lax.rem(me + k, devices)
        pl.semaphore_signal(barrier, inc=1, device_id=(to // n_col, lax.rem(to, n_col)),
                            device_id_type=MESH)

    nrow, ncol2, ch = wide.shape
    halves = ch // 128
    regions = shards.shape[1]
    bcols = ncol2 // 2
    level_size = nrow * ncol2
    levels = table.shape[1] // level_size
    col_base = lax.axis_index("col") * bcols

    level = 0
    for size in range(1, nrow + 1):
        while 2 ** (level + 1) <= size:
            level += 1
        lut[0, size] = level * level_size
        lut[1, size] = level * level_size - (2 ** level) * ncol2

    @pl.loop(0, nrow)
    def _(r):
        x = wide[r].astype(jnp.float32)
        for h in range(halves):
            table[h, pl.ds(pl.multiple_of(r * ncol2, 8), ncol2), :] = x[:, h * 128:(h + 1) * 128]

    for lv in range(1, levels):
        step = 2 ** (lv - 1)
        below = (lv - 1) * level_size
        count = nrow - 2 ** lv + 1

        @pl.loop(0, count)
        def _(r):
            for h in range(halves):
                one = table[h, pl.ds(pl.multiple_of(below + r * ncol2, 8), ncol2), :]
                two = table[h, pl.ds(pl.multiple_of(below + (r + step) * ncol2, 8), ncol2), :]
                table[h, pl.ds(pl.multiple_of(below + level_size + r * ncol2, 8), ncol2), :] = (
                    jnp.maximum(one, two))

    sub = lax.broadcasted_iota(jnp.int32, (8, 128), 0)

    def pool(n):
        r0, r1, c0, c1 = (boxes[k, n] for k in range(4))
        span = jnp.maximum(r1 - r0, 1)
        c0 = jnp.maximum(c0 - col_base, 0)
        c1 = c1 - col_base
        high = lut[0, span] + r0 * ncol2
        low = jnp.maximum(lut[1, span] + r1 * ncol2, 0)
        last = jnp.maximum(c1 - 8, c0)
        starts = [c0, jnp.minimum(c0 + 8, last), jnp.minimum(c0 + 16, last), last]
        inside = sub < c1 - c0
        for h in range(halves):
            got = [table[h, pl.ds(base + c, 8), :] for base in (high, low) for c in starts]
            while len(got) > 1:
                got = [jnp.maximum(got[k], got[k + 1]) for k in range(0, len(got), 2)]
            part[h, pl.ds(pl.multiple_of(n * 8, 8), 8), :] = jnp.where(inside, got[0], 0.0)

    @pl.loop(0, regions // 8)
    def _(g):
        for k in range(8):
            pool(g * 8 + k)

    pooled = jnp.concatenate(
        [
            functools.reduce(
                jnp.maximum, [part[h, pl.ds(s, regions, stride=8), :] for s in range(8)])
            for h in range(halves)
        ],
        axis=1,
    ).astype(jnp.bfloat16)

    ids = shards[...]
    same = (lax.broadcasted_iota(jnp.int32, (devices, regions), 0) == ids).astype(jnp.float32)
    early = (lax.broadcasted_iota(jnp.int32, (regions, regions), 0)
             < lax.broadcasted_iota(jnp.int32, (regions, regions), 1)).astype(jnp.float32)
    before = jnp.dot(same.astype(jnp.bfloat16), early.astype(jnp.bfloat16),
                     preferred_element_type=jnp.float32)
    slot = jnp.sum(before * same, axis=0, keepdims=True)
    target = ids * capacity + slot.astype(jnp.int32)
    size = 256
    for s in range(devices * capacity // size):
        place = lax.broadcasted_iota(jnp.int32, (size, regions), 0) + s * size
        pick = (place == target).astype(jnp.float32)
        filled = jnp.sum(pick, axis=1, keepdims=True)
        moved = jnp.dot(pick.astype(jnp.bfloat16), pooled, preferred_element_type=jnp.float32)
        moved = (moved + (filled - 1.0)).astype(src.dtype)
        group = size // capacity
        src[s * group:(s + 1) * group] = moved.reshape(group, capacity, ch)

    own = pltpu.make_async_copy(src.at[me], dst.at[me], own_sem)
    own.start()
    pl.semaphore_wait(barrier, devices - 1)

    def copy(k):
        to = lax.rem(me + k, devices)
        return pltpu.make_async_remote_copy(
            src_ref=src.at[to], dst_ref=dst.at[me],
            send_sem=send_sem.at[k], recv_sem=recv_sem.at[k],
            device_id=(to // n_col, lax.rem(to, n_col)), device_id_type=MESH)

    def got(k):
        away = lax.rem(me + devices - k, devices)
        return pltpu.make_async_remote_copy(
            src_ref=src.at[away], dst_ref=dst.at[away],
            send_sem=send_sem.at[k], recv_sem=recv_sem.at[k],
            device_id=(away // n_col, lax.rem(away, n_col)), device_id_type=MESH)

    @pl.loop(1, devices)
    def _(k):
        copy(k).start()

    own.wait()

    @pl.loop(1, devices)
    def _(k):
        copy(k).wait_send()
        got(k).wait_recv()


def describe_kernel(got, mean, weight, out):
    values = got[...].astype(jnp.float32)
    scale = lax.rsqrt(jnp.mean(values * values, axis=-1, keepdims=True) + EPSILON)
    centered = (values * scale - mean[...]).astype(jnp.bfloat16)
    white = jnp.dot(centered, weight[...], preferred_element_type=jnp.float32)
    scale = lax.rsqrt(jnp.mean(white * white, axis=-1, keepdims=True) + EPSILON)
    filled = values[:, 0:1] >= 0.0
    out[...] = jnp.where(filled, white * scale, 0.0).astype(out.dtype)


def body(n_row, n_col, features, conv_weight, conv_bias, boxes, shards, white_mean, white_weight):
    rows, cols, ch = features.shape
    layers = conv_weight.shape[0]
    devices = n_row * n_col
    regions = boxes.shape[-1]
    capacity = max(2, 2 * regions // devices)
    brows, bcols = rows // BLK, cols // BLK
    mid_w = cols + 16
    vmem = pl.BlockSpec(memory_space=pltpu.VMEM)
    any_spec = pl.BlockSpec(memory_space=pl.ANY)
    bf16 = jnp.bfloat16
    wide = pl.pallas_call(
        functools.partial(conv_kernel, n_row, n_col),
        out_shape=jax.ShapeDtypeStruct((n_row * brows, 2 * bcols, ch), bf16),
        in_specs=[any_spec, vmem, vmem],
        out_specs=vmem,
        scratch_shapes=[
            pltpu.VMEM((rows + 2 * layers, cols + 2 * PAD, ch), bf16),
            pltpu.VMEM((rows + 6, mid_w, 3 * ch), bf16),
            pltpu.VMEM((rows + 4, mid_w, 3 * ch), bf16),
            pltpu.VMEM((rows + 2, cols, 3 * ch), bf16),
            pltpu.VMEM((ch // 128, cols + 8, 128), jnp.float32),
            pltpu.SemaphoreType.DMA,
            pltpu.SemaphoreType.DMA((4,)),
            pltpu.SemaphoreType.DMA((4,)),
            pltpu.SemaphoreType.DMA((brows, 2 * n_row)),
            pltpu.SemaphoreType.DMA((brows, 2 * n_row)),
        ],
        compiler_params=pltpu.CompilerParams(
            collective_id=0, has_side_effects=True, vmem_limit_bytes=56 * 2**20),
    )(features, conv_weight.reshape(layers, 3, 3 * ch, ch), conv_bias)

    nbr = n_row * brows
    levels = nbr.bit_length()
    arrived = pl.pallas_call(
        functools.partial(pool_kernel, n_row, n_col),
        out_shape=jax.ShapeDtypeStruct((devices, capacity, ch), bf16),
        in_specs=[pl.BlockSpec(memory_space=pltpu.SMEM), vmem, vmem],
        out_specs=vmem,
        scratch_shapes=[
            pltpu.VMEM((devices, capacity, ch), bf16),
            pltpu.VMEM((ch // 128, levels * nbr * 2 * bcols, 128), jnp.float32),
            pltpu.VMEM((ch // 128, regions * 8 + 8, 128), jnp.float32),
            pltpu.SMEM((2, nbr + 1), jnp.int32),
            pltpu.SemaphoreType.DMA((devices,)),
            pltpu.SemaphoreType.DMA((devices,)),
            pltpu.SemaphoreType.DMA,
        ],
        compiler_params=pltpu.CompilerParams(
            collective_id=1, has_side_effects=True, vmem_limit_bytes=48 * 2**20),
    )(boxes.reshape(4, regions), shards.reshape(1, regions), wide)

    total = devices * capacity
    desc = white_weight.shape[1]
    block = 256
    return pl.pallas_call(
        describe_kernel,
        grid=(total // block,),
        out_shape=jax.ShapeDtypeStruct((total, desc), bf16),
        in_specs=[
            pl.BlockSpec((block, ch), lambda s: (s, 0)),
            pl.BlockSpec((1, ch), lambda s: (0, 0)),
            pl.BlockSpec((ch, desc), lambda s: (0, 0)),
        ],
        out_specs=pl.BlockSpec((block, desc), lambda s: (s, 0)),
        compiler_params=pltpu.CompilerParams(vmem_limit_bytes=32 * 2**20),
    )(arrived.reshape(total, ch), white_mean.reshape(1, ch), white_weight)


def solution(mesh):
    in_specs = (
        P("row", "col", None),
        P(),
        P(),
        P(None, "row", "col", None),
        P("row", "col", None, None),
        P(),
        P(),
    )
    out_specs = P(("row", "col"), None)
    part = functools.partial(body, mesh.shape["row"], mesh.shape["col"])
    return jax.shard_map(part, mesh=mesh, in_specs=in_specs, out_specs=out_specs, check_vma=False)
```
